32 devices in a mesh: blk: 4 (over z), group: 8 (over y, x, core).
Axes of the slice: x: 2, y: 2, z: 4, core: 2. Of those that a mesh axis runs over, the one named last changes fastest.
Arguments:
- positions: float32 [3, 262144], P(None, ('blk', 'group')), may hold values from -6 to 6
- velocities: float32 [3, 262144], P(None, ('blk', 'group')), may hold values from -6 to 6
- accelerations: float32 [3, 262144], P(None, ('blk', 'group')), may hold values from -6 to 6
- jerk_rates: float32 [3, 262144], P(None, ('blk', 'group')), may hold values from -24 to 24
- masses: float32 [262144], P(('blk', 'group')), may hold values from 0.1 to 10
- elapsed_time: float32 [262144], P(('blk', 'group')), may hold values from 0.05 to 0.5
- active_index: int32 [512], P(('blk', 'group')), may hold values from 0 to 262143
Outputs:
- new_pos: float32 [3, 512], P(None, ('blk', 'group'))
- new_vel: float32 [3, 512], P(None, ('blk', 'group'))
- new_acc: float32 [3, 512], P(None, ('blk', 'group'))
- new_jerk: float32 [3, 512], P(None, ('blk', 'group'))
The draws below stay inside these ranges and needn't reach their ends.
All inputs are finite; a program needn't handle non-finite values.
Results may differ from the reference program's by a relative error of at most 0.0003.
Values sent between devices are 32-bit elements; how exact they have to be, the bound alone decides.
A program may use at most 128 MiB of HBM per device.

```python
import math
import jax
import jax.numpy as jnp
import numpy as np
from jax import lax

STARS = 262144
ACTIVE = 512


def touch_ends(drawn, own_key, smallest, top_value):
    longest = drawn.shape.index(max(drawn.shape))
    spots = []
    for shift in (0, 1):
        where = [jax.random.randint(jax.random.fold_in(own_key, axis), (), 0, length) for axis, length in enumerate(drawn.shape)]
        where[longest] = (where[longest] + shift) % drawn.shape[longest]
        spots.append(tuple(where))
    return drawn.at[spots[0]].set(smallest).at[spots[1]].set(top_value)


def block_scale(stream_key, dims, split, low, top_value):
    factor_of = 1.0
    for dim, shards_of in split:
        steps = jax.random.uniform(jax.random.fold_in(jax.random.fold_in(stream_key, 6), dim), (shards_of,), jnp.float32, low / len(split), top_value / len(split))
        factor_of = factor_of * jnp.repeat(jnp.exp(steps), dims[dim] // shards_of).reshape((-1,) + (1,) * (len(dims) - 1 - dim))
    return factor_of


def skewed_wide(rng, dims, count, skew):
    weights = [min(1 << octave, count + 1 - (1 << octave)) * (1 << 20) // math.isqrt((1 << octave) ** skew) + 1 for octave in range((count + 1).bit_length()) if 1 << octave <= count]
    scale = 1 + sum(weights) // (1 << 30)
    listing = np.cumsum(np.array([max(1, weight // scale) for weight in weights]))
    lot = jax.random.randint(jax.random.fold_in(rng, 1), dims, 0, int(listing[len(weights) - 1]))
    start = jnp.left_shift(1, jnp.searchsorted(jnp.asarray(listing, jnp.int32), lot, side="right").astype(jnp.int32))
    grade = start - 1 + jax.random.randint(jax.random.fold_in(rng, 4), dims, 0, 1 << 30) % jnp.minimum(start, count + 1 - start)
    return jax.random.permutation(jax.random.fold_in(rng, 2), count)[grade].astype(jnp.int32)


def scatter_about(own_key, extent, deviation, bound, split=(), held_as=jnp.bfloat16):
    gain = block_scale(own_key, extent, split, -0.22, 0.18) if split else 1.0
    values = jax.random.normal(own_key, extent, jnp.float32) * deviation * gain
    return jnp.minimum(jnp.maximum(values, -bound), bound).astype(held_as)


def setup_inputs(seed: int = 0) -> dict:
    key_list = jax.random.split(jax.random.key(seed), 8)
    positions = scatter_about(key_list[0], (3, STARS), 1.0, 6.0, ((1, 32),), jnp.float32)
    velocities = scatter_about(key_list[1], (3, STARS), 1.0, 6.0, ((1, 32),), jnp.float32)
    accelerations = scatter_about(key_list[2], (3, STARS), 1.0, 6.0, ((1, 32),), jnp.float32)
    jerk_rates = scatter_about(key_list[3], (3, STARS), 4.0, 24.0, ((1, 32),), jnp.float32)
    masses = jnp.clip(jnp.exp(math.log(10.0) - 4.6051702 * jax.random.uniform(key_list[4], (STARS,), jnp.float32) ** block_scale(key_list[4], (STARS,), ((0, 32),), -0.2, 0.2)), 0.1, 10.0)
    elapsed_time = jnp.clip(jnp.exp(math.log(0.5) - 2.3025851 * jax.random.uniform(key_list[5], (STARS,), jnp.float32) ** block_scale(key_list[5], (STARS,), ((0, 32),), -0.2, 0.2)), 0.05, 0.5)
    active_index = touch_ends(skewed_wide(key_list[6], (ACTIVE,), STARS, 1), jax.random.fold_in(key_list[6], 3), 0, STARS - 1).astype(jnp.int32)
    return dict(positions=positions, velocities=velocities, accelerations=accelerations, jerk_rates=jerk_rates, masses=masses, elapsed_time=elapsed_time, active_index=active_index)


softening = 0.001

def predict(pos_now, vel_now, acc_now, jerk_now, elapsed):
    pred_pos = pos_now + elapsed * (vel_now + elapsed * (0.5 * acc_now + elapsed * (jerk_now / 6.0)))
    pred_vel = vel_now + elapsed * (acc_now + elapsed * (0.5 * jerk_now))
    return (pred_pos, pred_vel)

def block_forces(active_data, field_piece):
    offset = field_piece[0:3, None, :] - active_data[0:3, :, None]
    motion = field_piece[3:6, None, :] - active_data[3:6, :, None]
    dist_sq = lax.optimization_barrier(jnp.sum(offset * offset, axis=0)) + softening
    inverse = lax.rsqrt(dist_sq)
    weight = field_piece[6][None, :] * inverse * inverse * inverse
    factor = 3.0 * lax.optimization_barrier(jnp.sum(offset * motion, axis=0)) / dist_sq
    accel_part = lax.optimization_barrier(jnp.sum(offset * weight, axis=2))
    jerk_part = lax.optimization_barrier(jnp.sum((motion - factor * offset) * weight, axis=2))
    return jnp.concatenate([accel_part, jerk_part], axis=0)

def pair_forces(active_data, field):
    num_active = active_data.shape[1]
    num_field = field.shape[1]
    columns = math.gcd(num_field, max(1, 524288 // num_active))

    def advance(summed, which):
        field_piece = lax.dynamic_slice_in_dim(field, (which * columns).astype(jnp.int32), columns, 1)
        return (summed + block_forces(active_data, field_piece), None)
    summed, _ = lax.scan(advance, jnp.zeros((6, num_active), jnp.float32), jnp.arange(num_field // columns, dtype=jnp.int32))
    return summed

def corrector(owner_rows, forces):
    old_pos = owner_rows[0:3]
    old_vel = owner_rows[3:6]
    old_acc = owner_rows[6:9]
    old_jerk = owner_rows[9:12]
    elapsed = owner_rows[12]
    new_acc = forces[0:3]
    new_jerk = forces[3:6]
    squared = elapsed * elapsed / 12.0
    new_vel = old_vel + 0.5 * elapsed * (old_acc + new_acc) + squared * (old_jerk - new_jerk)
    new_pos = old_pos + 0.5 * elapsed * (old_vel + new_vel) + squared * (old_acc - new_acc)
    return (new_pos, new_vel, new_acc, new_jerk)

def active_state(owner_rows):
    pred_pos, pred_vel = predict(owner_rows[0:3], owner_rows[3:6], owner_rows[6:9], owner_rows[9:12], owner_rows[12])
    return jnp.concatenate([pred_pos, pred_vel], axis=0)

def reference(positions, velocities, accelerations, jerk_rates, masses, elapsed_time, active_index):
    pred_pos, pred_vel = predict(positions, velocities, accelerations, jerk_rates, elapsed_time)
    field = jnp.concatenate([pred_pos, pred_vel, masses[None, :]], axis=0)
    packed = jnp.concatenate([positions, velocities, accelerations, jerk_rates, elapsed_time[None, :]], axis=0)
    owner_rows = jnp.take(packed, active_index.astype(jnp.int32), axis=1)
    forces = pair_forces(active_state(owner_rows), field) * (1.0 / STARS)
    return corrector(owner_rows, forces)
```

```python
import functools

import jax
import jax.numpy as jnp
from jax import lax
from jax.experimental import pallas as pl
from jax.experimental.pallas import tpu as pltpu
from jax.sharding import PartitionSpec as P

softening = 0.001
MESH = pl.DeviceIdType.MESH
F32 = jnp.float32
BF16 = jnp.bfloat16
LANES = 128
CHUNK = 256
ROWS = 512
PARTS = ((0, 0), (0, 1), (1, 0), (0, 2), (2, 0), (1, 1))
NT = (((1,), (1,)), ((), ()))


def predict(pos_now, vel_now, acc_now, jerk_now, elapsed):
    pred_pos = pos_now + elapsed * (
        vel_now + elapsed * (0.5 * acc_now + elapsed * (jerk_now / 6.0))
    )
    pred_vel = vel_now + elapsed * (acc_now + elapsed * (0.5 * jerk_now))
    return (pred_pos, pred_vel)


def split3(value):
    high = value.astype(BF16).astype(F32)
    rest = value - high
    middle = rest.astype(BF16).astype(F32)
    low = (rest - middle).astype(BF16).astype(F32)
    return (high, middle, low)


def padded(pieces, rows):
    have = sum(piece.shape[0] for piece in pieces)
    width = pieces[0].shape[1]
    if have < rows:
        pieces = list(pieces) + [jnp.zeros((rows - have, width), F32)]
    return jnp.concatenate(pieces, axis=0)


def kernel(
    blocks, groups, total_stars,
    pos_ref, vel_ref, acc_ref, jerk_ref, mass_ref, time_ref, index_ref,
    out_pos, out_vel, out_acc, out_jerk,
    index_all, index_col, packed, field_u, field_s, motion_rhs, field_pos,
    picked, send_state, recv_state, state_all, state, rows_lhs, rows_pos,
    weights_a, weights_b, sums, send_force, recv_force,
    send_sem, recv_sem,
):
    devices = blocks * groups
    own_stars = pos_ref.shape[1]
    own_active = index_ref.shape[1]
    active = devices * own_active
    lane_blocks = active // LANES
    per_block = LANES // own_active
    me = lax.axis_index("blk") * groups + lax.axis_index("group")

    def peer_of(step):
        peer = lax.rem(me + step, devices)
        return peer, (peer // groups, lax.rem(peer, groups))

    barrier = pltpu.get_barrier_semaphore()

    def greet(step, carry):
        pl.semaphore_signal(barrier, inc=1, device_id=peer_of(step)[1], device_id_type=MESH)
        return carry

    lax.fori_loop(1, devices, greet, 0)

    def exchange(phase, source, target):
        def copy_to(step):
            peer, where = peer_of(step)
            return pltpu.make_async_remote_copy(
                src_ref=source(peer),
                dst_ref=target.at[me],
                send_sem=send_sem.at[phase, step],
                recv_sem=recv_sem.at[phase, me],
                device_id=where,
                device_id_type=MESH,
            )

        def start(step, carry):
            copy_to(step).start()
            return carry

        def finish(step, carry):
            sender = lax.rem(me + step, devices)
            pltpu.make_async_remote_copy(
                src_ref=source(sender),
                dst_ref=target.at[sender],
                send_sem=send_sem.at[phase, step],
                recv_sem=recv_sem.at[phase, sender],
                device_id=peer_of(step)[1],
                device_id_type=MESH,
            ).wait()
            return carry

        lax.fori_loop(1, devices, start, 0)
        return lambda: lax.fori_loop(1, devices, finish, 0)

    index_row = jnp.concatenate(
        [index_ref[...], jnp.zeros((1, LANES - own_active), jnp.int32)], axis=1
    )
    index_all[me] = index_row
    pl.semaphore_wait(barrier, devices - 1)
    finish_index = exchange(0, lambda peer: index_all.at[me], index_all)

    piece = 1024

    def prepare(which, carry):
        at = pl.ds(pl.multiple_of(which * piece, piece), piece)
        old_pos, old_vel, old_acc, old_jerk = (
            ref[:, at] for ref in (pos_ref, vel_ref, acc_ref, jerk_ref)
        )
        mass, elapsed = mass_ref[:, at], time_ref[:, at]
        pred_pos, pred_vel = predict(old_pos, old_vel, old_acc, old_jerk, elapsed)
        rows = padded([old_pos, old_vel, old_acc, old_jerk, elapsed], 16)
        packed[:, at] = padded(split3(rows), LANES).astype(BF16)
        field_pos[:, at] = padded([pred_pos], 8)
        moments = padded([mass * pred_pos, mass * pred_vel, mass], 8)
        split = jnp.concatenate(split3(moments), axis=0)
        field_u[:, at] = padded([split], LANES).astype(BF16)
        field_s[:, at] = padded([jnp.zeros((32, piece), F32), split], LANES).astype(BF16)
        pos_parts, vel_parts = split3(pred_pos), split3(pred_vel)
        dot_parts = split3(jnp.sum(pred_pos * pred_vel, axis=0, keepdims=True))
        ones = jnp.ones((1, piece), F32)
        rhs = [pos_parts[right] for _, right in PARTS] + [vel_parts[right] for _, right in PARTS]
        motion_rhs[:, at] = padded(rhs + list(dot_parts) + [ones] * 3, LANES).astype(BF16)
        return carry

    lax.fori_loop(0, own_stars // piece, prepare, 0)

    finish_index()
    first = me * own_stars
    local = (index_all[...].reshape(devices, LANES) - first).astype(F32)
    local = jnp.transpose(local)
    for device in range(devices):
        column = local[:own_active, device : device + 1]
        index_col[device * own_active : (device + 1) * own_active, :] = jnp.broadcast_to(
            column, (own_active, LANES)
        )

    wide = 512
    tile = min(ROWS, active)

    for block in range(active // tile):
        picked[block * tile : (block + 1) * tile, :] = jnp.zeros((tile, LANES), F32)

        def pick(which, carry):
            base = which * wide
            at = pl.ds(pl.multiple_of(base, wide), wide)
            lanes = lax.broadcasted_iota(jnp.int32, (1, wide), 1) + base
            lanes = lanes.astype(F32)
            pieces = []
            for part in range(wide // LANES):
                column = index_col[block * tile : (block + 1) * tile, :]
                same = column == lanes[:, part * LANES : (part + 1) * LANES]
                pieces.append(jnp.where(same, 1.0, 0.0).astype(BF16))
            chosen = jnp.concatenate(pieces, axis=1)
            picked[block * tile : (block + 1) * tile, :] += lax.dot_general(
                chosen, packed[:, at], NT, preferred_element_type=F32
            )
            return carry

        lax.fori_loop(0, own_stars // wide, pick, 0)

    for block in range(lane_blocks):
        turned = jnp.transpose(picked[block * LANES : (block + 1) * LANES, :])
        rows = turned[0:16] + turned[16:32] + turned[32:48]
        for pair in range(per_block):
            send_state[block * per_block + pair] = rows[2 * pair : 2 * pair + 2]
    recv_state[me] = send_state[me]
    exchange(1, lambda peer: send_state.at[peer], recv_state)()
    state_all[me] = jnp.sum(recv_state[...], axis=0)
    exchange(2, lambda peer: state_all.at[me], state_all)()

    for block in range(lane_blocks):
        for pair in range(per_block):
            state[block, 2 * pair : 2 * pair + 2, :] = state_all[block * per_block + pair]
    for block in range(lane_blocks):
        rows = state[block]
        pred_pos, pred_vel = predict(rows[0:3], rows[3:6], rows[6:9], rows[9:12], rows[12:13])
        pos_parts, vel_parts = split3(-pred_pos), split3(-pred_vel)
        dot_parts = split3(jnp.sum(pred_pos * pred_vel, axis=0, keepdims=True))
        ones = jnp.ones((1, LANES), F32)
        lhs = [vel_parts[left] for left, _ in PARTS] + [pos_parts[left] for left, _ in PARTS]
        lhs = jnp.transpose(padded(lhs + [ones] * 3 + list(dot_parts), LANES))
        rows_lhs[block * LANES : (block + 1) * LANES, :] = lhs.astype(BF16)
        columns = jnp.transpose(padded([pred_pos], LANES))
        for axis in range(3):
            rows_pos[axis, block * LANES : (block + 1) * LANES, :] = jnp.broadcast_to(
                columns[:, axis : axis + 1], (LANES, LANES)
            )

    chunks = own_stars // CHUNK

    def pair_weights(first_row, which, target):
        at = pl.ds(pl.multiple_of(which * CHUNK, CHUNK), CHUNK)
        stars = [field_pos[axis : axis + 1, at] for axis in range(3)]
        along = jnp.dot(
            rows_lhs[pl.ds(first_row, tile), :], motion_rhs[:, at], preferred_element_type=F32
        )
        high = 16
        for row in range(0, tile, high):
            mine = [rows_pos[axis, pl.ds(first_row + row, high), :] for axis in range(3)]
            for lane in range(0, CHUNK, LANES):
                squares = []
                for axis in range(3):
                    offset = stars[axis][:, lane : lane + LANES] - mine[axis]
                    squares.append(offset * offset)
                inverse = lax.rsqrt(squares[0] + squares[1] + squares[2] + softening)
                inverse_sq = inverse * inverse
                cubed = inverse_sq * inverse
                slope = cubed * (inverse_sq * along[row : row + high, lane : lane + LANES])
                for number, value in enumerate((cubed, slope)):
                    near = value.astype(BF16)
                    far = (value - near.astype(F32)).astype(BF16)
                    start = 2 * number * CHUNK + lane
                    target[row : row + high, start : start + LANES] = near
                    start += CHUNK
                    target[row : row + high, start : start + LANES] = far

    def add_up(first_row, which, source):
        at = pl.ds(pl.multiple_of(which * CHUNK, CHUNK), CHUNK)
        near, far = field_u[:, at], field_s[:, at]
        field = jnp.concatenate([near, near, far, far], axis=1)
        sums[pl.ds(first_row, tile), :] += lax.dot_general(
            source[...], field, NT, preferred_element_type=F32
        )

    for block in range(active // tile):
        first_row = block * tile
        sums[pl.ds(first_row, tile), :] = jnp.zeros((tile, LANES), F32)
        pair_weights(first_row, 0, weights_a)

        def advance(which, carry):
            pair_weights(first_row, 2 * which + 1, weights_b)
            add_up(first_row, 2 * which, weights_a)
            pair_weights(first_row, lax.rem(2 * which + 2, chunks), weights_a)
            add_up(first_row, 2 * which + 1, weights_b)
            return carry

        lax.fori_loop(0, chunks // 2, advance, 0)

    gravity = 1.0 / total_stars
    for block in range(lane_blocks):
        turned = jnp.transpose(sums[block * LANES : (block + 1) * LANES, :])
        plain = turned[0:8] + turned[8:16] + turned[16:24]
        sloped = turned[32:40] + turned[40:48] + turned[48:56]
        rows = state[block]
        pred_pos, pred_vel = predict(rows[0:3], rows[3:6], rows[6:9], rows[9:12], rows[12:13])
        accel = plain[0:3] - pred_pos * plain[6:7]
        jerk = (plain[3:6] - pred_vel * plain[6:7]) - 3.0 * (
            sloped[0:3] - pred_pos * sloped[6:7]
        )
        send_force[block] = padded([accel, jerk], 8)
    mine = me // per_block
    recv_force[me] = send_force[mine]
    exchange(3, lambda peer: send_force.at[peer // per_block], recv_force)()
    forces = jnp.sum(recv_force[...], axis=0) * gravity
    rows = state[mine]
    shift = lax.rem(LANES - own_active * lax.rem(me, per_block), LANES)
    forces = pltpu.roll(forces, shift, 1)
    rows = pltpu.roll(rows, shift, 1)
    new_acc, new_jerk = forces[0:3], forces[3:6]
    old_pos, old_vel, old_acc, old_jerk = rows[0:3], rows[3:6], rows[6:9], rows[9:12]
    elapsed = rows[12:13]
    squared = elapsed * elapsed / 12.0
    new_vel = old_vel + 0.5 * elapsed * (old_acc + new_acc) + squared * (old_jerk - new_jerk)
    new_pos = old_pos + 0.5 * elapsed * (old_vel + new_vel) + squared * (old_acc - new_acc)
    out_pos[...] = new_pos[:, :own_active]
    out_vel[...] = new_vel[:, :own_active]
    out_acc[...] = new_acc[:, :own_active]
    out_jerk[...] = new_jerk[:, :own_active]


def solution(mesh):
    blocks, groups = mesh.shape["blk"], mesh.shape["group"]
    devices = blocks * groups

    def on_device(positions, velocities, accelerations, jerk_rates, masses, elapsed_time, active_index):
        own_stars = positions.shape[1]
        own_active = active_index.shape[0]
        active = devices * own_active
        lane_blocks = active // LANES
        tile = min(ROWS, active)
        out = jax.ShapeDtypeStruct((3, own_active), F32)
        vmem = pl.BlockSpec(memory_space=pltpu.VMEM)
        return pl.pallas_call(
            functools.partial(kernel, blocks, groups, own_stars * devices),
            out_shape=(out,) * 4,
            in_specs=[vmem] * 7,
            out_specs=(vmem,) * 4,
            scratch_shapes=[
                pltpu.VMEM((devices, 1, LANES), jnp.int32),
                pltpu.VMEM((active, LANES), F32),
                pltpu.VMEM((LANES, own_stars), BF16),
                pltpu.VMEM((LANES, own_stars), BF16),
                pltpu.VMEM((LANES, own_stars), BF16),
                pltpu.VMEM((LANES, own_stars), BF16),
                pltpu.VMEM((8, own_stars), F32),
                pltpu.VMEM((active, LANES), F32),
                pltpu.VMEM((devices, 2, LANES), F32),
                pltpu.VMEM((devices, 2, LANES), F32),
                pltpu.VMEM((devices, 2, LANES), F32),
                pltpu.VMEM((lane_blocks, 16, LANES), F32),
                pltpu.VMEM((active, LANES), BF16),
                pltpu.VMEM((3, active, LANES), F32),
                pltpu.VMEM((tile, 4 * CHUNK), BF16),
                pltpu.VMEM((tile, 4 * CHUNK), BF16),
                pltpu.VMEM((active, LANES), F32),
                pltpu.VMEM((lane_blocks, 8, LANES), F32),
                pltpu.VMEM((devices, 8, LANES), F32),
                pltpu.SemaphoreType.DMA((4, devices)),
                pltpu.SemaphoreType.DMA((4, devices)),
            ],
            compiler_params=pltpu.CompilerParams(
                collective_id=0, has_side_effects=True, vmem_limit_bytes=40 * 1024 * 1024
            ),
            cost_estimate=pl.CostEstimate(
                flops=40 * active * own_stars, bytes_accessed=4 * 14 * own_stars,
                transcendentals=active * own_stars,
            ),
        )(
            positions, velocities, accelerations, jerk_rates,
            masses.reshape(1, own_stars), elapsed_time.reshape(1, own_stars),
            active_index.reshape(1, own_active),
        )

    wide = P(None, ("blk", "group"))
    flat = P(("blk", "group"))
    return jax.shard_map(
        on_device,
        mesh=mesh,
        in_specs=(wide, wide, wide, wide, flat, flat, flat),
        out_specs=(wide,) * 4,
        check_vma=False,
    )
```

```python
import functools

import jax
import jax.numpy as jnp
from jax import lax
from jax.experimental import pallas as pl
from jax.experimental.pallas import tpu as pltpu
from jax.sharding import PartitionSpec as P

softening = 0.001
MESH = pl.DeviceIdType.MESH
F32 = jnp.float32
BF16 = jnp.bfloat16
LANES = 128
CHUNK = 512
DEEP = 64
ROWS = 512
PARTS = ((0, 0), (0, 1), (1, 0), (0, 2), (2, 0), (1, 1))
NT = (((1,), (1,)), ((), ()))


def predict(pos_now, vel_now, acc_now, jerk_now, elapsed):
    pred_pos = pos_now + elapsed * (
        vel_now + elapsed * (0.5 * acc_now + elapsed * (jerk_now / 6.0))
    )
    pred_vel = vel_now + elapsed * (acc_now + elapsed * (0.5 * jerk_now))
    return (pred_pos, pred_vel)


def split3(value):
    high = value.astype(BF16).astype(F32)
    rest = value - high
    middle = rest.astype(BF16).astype(F32)
    low = (rest - middle).astype(BF16).astype(F32)
    return (high, middle, low)


def padded(pieces, rows):
    have = sum(piece.shape[0] for piece in pieces)
    width = pieces[0].shape[1]
    if have < rows:
        pieces = list(pieces) + [jnp.zeros((rows - have, width), F32)]
    return jnp.concatenate(pieces, axis=0)


def kernel(
    blocks, groups, total_stars,
    pos_hbm, vel_hbm, acc_hbm, jerk_hbm, mass_hbm, time_hbm, index_hbm,
    result,
    pos_ref, vel_ref, acc_ref, jerk_ref, mass_ref, time_ref, index_ref,
    index_all, index_col, packed, field_u, field_s, motion_rhs, field_pos,
    picked, send_state, recv_state, state_all, state, rows_lhs, rows_pos,
    weights_a, weights_b, sums, send_force, recv_force,
    send_sem, recv_sem, load_sem,
):
    loads = [
        pltpu.make_async_copy(far, near, load_sem.at[number])
        for number, (far, near) in enumerate((
            (index_hbm, index_ref), (pos_hbm, pos_ref), (vel_hbm, vel_ref), (acc_hbm, acc_ref),
            (jerk_hbm, jerk_ref), (mass_hbm, mass_ref), (time_hbm, time_ref),
        ))
    ]
    for load in loads:
        load.start()
    devices = blocks * groups
    own_stars = pos_ref.shape[1]
    own_active = index_ref.shape[1]
    active = devices * own_active
    lane_blocks = active // LANES
    per_block = LANES // own_active
    me = lax.axis_index("blk") * groups + lax.axis_index("group")

    def peer_of(step):
        peer = lax.rem(me + step, devices)
        return peer, (peer // groups, lax.rem(peer, groups))

    barrier = pltpu.get_barrier_semaphore()

    def greet(step, carry):
        pl.semaphore_signal(barrier, inc=1, device_id=peer_of(step)[1], device_id_type=MESH)
        return carry

    lax.fori_loop(1, devices, greet, 0, unroll=True)

    def exchange(phase, source, target):
        def start(step, carry):
            peer, where = peer_of(step)
            pltpu.make_async_remote_copy(
                src_ref=source(peer),
                dst_ref=target.at[me],
                send_sem=send_sem.at[phase],
                recv_sem=recv_sem.at[phase],
                device_id=where,
                device_id_type=MESH,
            ).start()
            return carry

        lax.fori_loop(1, devices, start, 0, unroll=True)

        def finish():
            every = target.at[pl.ds(0, devices - 1)]
            pltpu.make_async_copy(every, every, send_sem.at[phase]).wait()
            pltpu.make_async_copy(every, every, recv_sem.at[phase]).wait()

        return finish

    loads[0].wait()
    index_row = jnp.concatenate(
        [index_ref[...], jnp.zeros((1, LANES - own_active), jnp.int32)], axis=1
    )
    index_all[me] = index_row
    pl.semaphore_wait(barrier, devices - 1)
    finish_index = exchange(0, lambda peer: index_all.at[me], index_all)

    for load in loads[1:]:
        load.wait()
    piece = 1024

    def prepare(which, carry):
        at = pl.ds(pl.multiple_of(which * piece, piece), piece)
        old_pos, old_vel, old_acc, old_jerk = (
            ref[:, at] for ref in (pos_ref, vel_ref, acc_ref, jerk_ref)
        )
        mass, elapsed = mass_ref[:, at], time_ref[:, at]
        pred_pos, pred_vel = predict(old_pos, old_vel, old_acc, old_jerk, elapsed)
        rows = padded([old_pos, old_vel, old_acc, old_jerk, elapsed], 16)
        packed[:, at] = padded(split3(rows), DEEP).astype(BF16)
        field_pos[:, at] = padded([pred_pos], 8)
        moments = padded([mass * pred_pos, mass * pred_vel, mass], 8)
        split = jnp.concatenate(split3(moments), axis=0)
        field_u[:, at] = padded([split], DEEP).astype(BF16)
        field_s[:, at] = padded([jnp.zeros((32, piece), F32), split], DEEP).astype(BF16)
        pos_parts, vel_parts = split3(pred_pos), split3(pred_vel)
        dot_parts = split3(jnp.sum(pred_pos * pred_vel, axis=0, keepdims=True))
        ones = jnp.ones((1, piece), F32)
        rhs = [pos_parts[right] for _, right in PARTS] + [vel_parts[right] for _, right in PARTS]
        motion_rhs[:, at] = padded(rhs + list(dot_parts) + [ones] * 3, DEEP).astype(BF16)
        return carry

    lax.fori_loop(0, own_stars // piece, prepare, 0)

    finish_index()
    first = me * own_stars
    local = (index_all[...].reshape(devices, LANES) - first).astype(F32)
    local = jnp.transpose(local)
    for device in range(devices):
        column = local[:own_active, device : device + 1]
        index_col[device * own_active : (device + 1) * own_active, :] = jnp.broadcast_to(
            column, (own_active, LANES)
        )

    wide = 512
    tile = min(ROWS, active)

    for block in range(active // tile):
        picked[block * tile : (block + 1) * tile, :] = jnp.zeros((tile, DEEP), F32)

        def pick(which, carry):
            base = which * wide
            at = pl.ds(pl.multiple_of(base, wide), wide)
            lanes = lax.broadcasted_iota(jnp.int32, (1, wide), 1) + base
            lanes = lanes.astype(F32)
            pieces = []
            for part in range(wide // LANES):
                column = index_col[block * tile : (block + 1) * tile, :]
                same = column == lanes[:, part * LANES : (part + 1) * LANES]
                pieces.append(jnp.where(same, 1.0, 0.0).astype(BF16))
            chosen = jnp.concatenate(pieces, axis=1)
            picked[block * tile : (block + 1) * tile, :] += lax.dot_general(
                chosen, packed[:, at], NT, preferred_element_type=F32
            )
            return carry

        lax.fori_loop(0, own_stars // wide, pick, 0)

    for block in range(lane_blocks):
        turned = jnp.transpose(picked[block * LANES : (block + 1) * LANES, :])
        rows = turned[0:16] + turned[16:32] + turned[32:48]
        for pair in range(per_block):
            send_state[block * per_block + pair] = rows[2 * pair : 2 * pair + 2]
    recv_state[me] = send_state[me]
    exchange(1, lambda peer: send_state.at[peer], recv_state)()
    state_all[me] = jnp.sum(recv_state[...], axis=0)
    exchange(2, lambda peer: state_all.at[me], state_all)()

    for block in range(lane_blocks):
        for pair in range(per_block):
            state[block, 2 * pair : 2 * pair + 2, :] = state_all[block * per_block + pair]
    for block in range(lane_blocks):
        rows = state[block]
        pred_pos, pred_vel = predict(rows[0:3], rows[3:6], rows[6:9], rows[9:12], rows[12:13])
        pos_parts, vel_parts = split3(-pred_pos), split3(-pred_vel)
        dot_parts = split3(jnp.sum(pred_pos * pred_vel, axis=0, keepdims=True))
        ones = jnp.ones((1, LANES), F32)
        lhs = [vel_parts[left] for left, _ in PARTS] + [pos_parts[left] for left, _ in PARTS]
        lhs = jnp.transpose(padded(lhs + [ones] * 3 + list(dot_parts), LANES))
        rows_lhs[block * LANES : (block + 1) * LANES, :] = lhs[:, :DEEP].astype(BF16)
        columns = jnp.transpose(padded([pred_pos], LANES))
        for axis in range(3):
            rows_pos[axis, block * LANES : (block + 1) * LANES, :] = jnp.broadcast_to(
                columns[:, axis : axis + 1], (LANES, LANES)
            )

    chunks = own_stars // CHUNK

    def pair_weights(first_row, which, target):
        at = pl.ds(pl.multiple_of(which * CHUNK, CHUNK), CHUNK)
        stars = [field_pos[axis : axis + 1, at] for axis in range(3)]
        along = jnp.dot(
            rows_lhs[pl.ds(first_row, tile), :], motion_rhs[:, at], preferred_element_type=F32
        )
        high = 16
        for row in range(0, tile, high):
            mine = [rows_pos[axis, pl.ds(first_row + row, high), :] for axis in range(3)]
            for lane in range(0, CHUNK, LANES):
                squares = []
                for axis in range(3):
                    offset = stars[axis][:, lane : lane + LANES] - mine[axis]
                    squares.append(offset * offset)
                inverse = lax.rsqrt(squares[0] + squares[1] + squares[2] + softening)
                inverse_sq = inverse * inverse
                cubed = inverse_sq * inverse
                slope = cubed * (inverse_sq * along[row : row + high, lane : lane + LANES])
                for number, value in enumerate((cubed, slope)):
                    near = value.astype(BF16)
                    far = (value - near.astype(F32)).astype(BF16)
                    start = 2 * number * CHUNK + lane
                    target[row : row + high, start : start + LANES] = near
                    start += CHUNK
                    target[row : row + high, start : start + LANES] = far

    def add_up(first_row, which, source):
        at = pl.ds(pl.multiple_of(which * CHUNK, CHUNK), CHUNK)
        near, far = field_u[:, at], field_s[:, at]
        field = jnp.concatenate([near, near, far, far], axis=1)
        half = tile // 2
        for part in range(2):
            rows = pl.ds(first_row + part * half, half)
            sums[rows, :] += lax.dot_general(
                source[part * half : (part + 1) * half, :], field, NT, preferred_element_type=F32
            )

    for block in range(active // tile):
        first_row = block * tile
        sums[pl.ds(first_row, tile), :] = jnp.zeros((tile, DEEP), F32)
        pair_weights(first_row, 0, weights_a)

        def advance(which, carry):
            pair_weights(first_row, 2 * which + 1, weights_b)
            add_up(first_row, 2 * which, weights_a)
            pair_weights(first_row, lax.rem(2 * which + 2, chunks), weights_a)
            add_up(first_row, 2 * which + 1, weights_b)
            return carry

        lax.fori_loop(0, chunks // 2, advance, 0)

    gravity = 1.0 / total_stars
    for block in range(lane_blocks):
        turned = jnp.transpose(sums[block * LANES : (block + 1) * LANES, :])
        plain = turned[0:8] + turned[8:16] + turned[16:24]
        sloped = turned[32:40] + turned[40:48] + turned[48:56]
        rows = state[block]
        pred_pos, pred_vel = predict(rows[0:3], rows[3:6], rows[6:9], rows[9:12], rows[12:13])
        accel = plain[0:3] - pred_pos * plain[6:7]
        jerk = (plain[3:6] - pred_vel * plain[6:7]) - 3.0 * (
            sloped[0:3] - pred_pos * sloped[6:7]
        )
        send_force[block] = padded([accel, jerk], 8)
    mine = me // per_block
    recv_force[me] = send_force[mine]
    exchange(3, lambda peer: send_force.at[peer // per_block], recv_force)()
    forces = jnp.sum(recv_force[...], axis=0) * gravity
    rows = state[mine]
    shift = lax.rem(LANES - own_active * lax.rem(me, per_block), LANES)
    forces = pltpu.roll(forces, shift, 1)
    rows = pltpu.roll(rows, shift, 1)
    new_acc, new_jerk = forces[0:3], forces[3:6]
    old_pos, old_vel, old_acc, old_jerk = rows[0:3], rows[3:6], rows[6:9], rows[9:12]
    elapsed = rows[12:13]
    squared = elapsed * elapsed / 12.0
    new_vel = old_vel + 0.5 * elapsed * (old_acc + new_acc) + squared * (old_jerk - new_jerk)
    new_pos = old_pos + 0.5 * elapsed * (old_vel + new_vel) + squared * (old_acc - new_acc)
    for number, value in enumerate((new_pos, new_vel, new_acc, new_jerk)):
        result[number] = value[:, :own_active]


def hand_out(result, out_pos, out_vel, out_acc, out_jerk):
    for number, out in enumerate((out_pos, out_vel, out_acc, out_jerk)):
        out[...] = result[number]


def solution(mesh):
    blocks, groups = mesh.shape["blk"], mesh.shape["group"]
    devices = blocks * groups

    def on_device(positions, velocities, accelerations, jerk_rates, masses, elapsed_time, active_index):
        own_stars = positions.shape[1]
        own_active = active_index.shape[0]
        active = devices * own_active
        lane_blocks = active // LANES
        tile = min(ROWS, active)
        out = jax.ShapeDtypeStruct((3, own_active), F32)
        vmem = pl.BlockSpec(memory_space=pltpu.VMEM)
        result = pl.pallas_call(
            functools.partial(kernel, blocks, groups, own_stars * devices),
            out_shape=jax.ShapeDtypeStruct((4, 3, own_active), F32),
            in_specs=[pl.BlockSpec(memory_space=pltpu.HBM)] * 7,
            out_specs=vmem,
            scratch_shapes=[
                pltpu.VMEM((3, own_stars), F32),
                pltpu.VMEM((3, own_stars), F32),
                pltpu.VMEM((3, own_stars), F32),
                pltpu.VMEM((3, own_stars), F32),
                pltpu.VMEM((1, own_stars), F32),
                pltpu.VMEM((1, own_stars), F32),
                pltpu.VMEM((1, own_active), jnp.int32),
                pltpu.VMEM((devices, 1, LANES), jnp.int32),
                pltpu.VMEM((active, LANES), F32),
                pltpu.VMEM((DEEP, own_stars), BF16),
                pltpu.VMEM((DEEP, own_stars), BF16),
                pltpu.VMEM((DEEP, own_stars), BF16),
                pltpu.VMEM((DEEP, own_stars), BF16),
                pltpu.VMEM((8, own_stars), F32),
                pltpu.VMEM((active, DEEP), F32),
                pltpu.VMEM((devices, 2, LANES), F32),
                pltpu.VMEM((devices, 2, LANES), F32),
                pltpu.VMEM((devices, 2, LANES), F32),
                pltpu.VMEM((lane_blocks, 16, LANES), F32),
                pltpu.VMEM((active, DEEP), BF16),
                pltpu.VMEM((3, active, LANES), F32),
                pltpu.VMEM((tile, 4 * CHUNK), BF16),
                pltpu.VMEM((tile, 4 * CHUNK), BF16),
                pltpu.VMEM((active, DEEP), F32),
                pltpu.VMEM((lane_blocks, 8, LANES), F32),
                pltpu.VMEM((devices, 8, LANES), F32),
                pltpu.SemaphoreType.DMA((4,)),
                pltpu.SemaphoreType.DMA((4,)),
                pltpu.SemaphoreType.DMA((7,)),
            ],
            compiler_params=pltpu.CompilerParams(
                collective_id=0, has_side_effects=True, vmem_limit_bytes=56 * 1024 * 1024
            ),
            cost_estimate=pl.CostEstimate(
                flops=40 * active * own_stars, bytes_accessed=4 * 14 * own_stars,
                transcendentals=active * own_stars,
            ),
        )(
            positions, velocities, accelerations, jerk_rates,
            masses.reshape(1, own_stars), elapsed_time.reshape(1, own_stars),
            active_index.reshape(1, own_active),
        )
        return pl.pallas_call(
            hand_out, out_shape=(out,) * 4, in_specs=[vmem], out_specs=(vmem,) * 4
        )(result)

    wide = P(None, ("blk", "group"))
    flat = P(("blk", "group"))
    return jax.shard_map(
        on_device,
        mesh=mesh,
        in_specs=(wide, wide, wide, wide, flat, flat, flat),
        out_specs=(wide,) * 4,
        check_vma=False,
    )
```

```python
import functools

import jax
import jax.numpy as jnp
from jax import lax
from jax.experimental import pallas as pl
from jax.experimental.pallas import tpu as pltpu
from jax.sharding import PartitionSpec as P

softening = 0.001
MESH = pl.DeviceIdType.MESH
F32 = jnp.float32
BF16 = jnp.bfloat16
LANES = 128
CHUNK = 256
DEEP = 64
ROWS = 512
PARTS = ((0, 0), (0, 1), (1, 0), (0, 2), (2, 0), (1, 1))


def predict(pos_now, vel_now, acc_now, jerk_now, elapsed):
    pred_pos = pos_now + elapsed * (
        vel_now + elapsed * (0.5 * acc_now + elapsed * (jerk_now / 6.0))
    )
    pred_vel = vel_now + elapsed * (acc_now + elapsed * (0.5 * jerk_now))
    return (pred_pos, pred_vel)


def split3(value):
    high = value.astype(BF16).astype(F32)
    rest = value - high
    middle = rest.astype(BF16).astype(F32)
    low = (rest - middle).astype(BF16).astype(F32)
    return (high, middle, low)


def padded(pieces, rows):
    have = sum(piece.shape[0] for piece in pieces)
    width = pieces[0].shape[1]
    if have < rows:
        pieces = list(pieces) + [jnp.zeros((rows - have, width), F32)]
    return jnp.concatenate(pieces, axis=0)


def kernel(
    blocks, groups, total_stars,
    pos_hbm, vel_hbm, acc_hbm, jerk_hbm, mass_hbm, time_hbm, index_hbm,
    result,
    pos_ref, vel_ref, acc_ref, jerk_ref, mass_ref, time_ref, index_ref,
    index_all, packed, field, motion_lhs, star_pos,
    picked, send_state, recv_state, state_all, state, rows_rhs, rows_pos,
    weights_a, weights_b, sums, send_force, recv_force,
    send_sem, recv_sem, load_sem,
):
    loads = [
        pltpu.make_async_copy(far, near, load_sem.at[number])
        for number, (far, near) in enumerate((
            (index_hbm, index_ref), (pos_hbm, pos_ref), (vel_hbm, vel_ref), (acc_hbm, acc_ref),
            (jerk_hbm, jerk_ref), (mass_hbm, mass_ref), (time_hbm, time_ref),
        ))
    ]
    for load in loads:
        load.start()
    devices = blocks * groups
    own_stars = pos_ref.shape[1]
    own_active = index_ref.shape[1]
    active = devices * own_active
    lane_blocks = active // LANES
    per_block = LANES // own_active
    me = lax.axis_index("blk") * groups + lax.axis_index("group")

    def peer_of(step):
        peer = lax.rem(me + step, devices)
        return peer, (peer // groups, lax.rem(peer, groups))

    barrier = pltpu.get_barrier_semaphore()

    def greet(step, carry):
        pl.semaphore_signal(barrier, inc=1, device_id=peer_of(step)[1], device_id_type=MESH)
        return carry

    lax.fori_loop(1, devices, greet, 0, unroll=True)

    def exchange(phase, source, target):
        def start(step, carry):
            peer, where = peer_of(step)
            pltpu.make_async_remote_copy(
                src_ref=source(peer),
                dst_ref=target.at[me],
                send_sem=send_sem.at[phase],
                recv_sem=recv_sem.at[phase],
                device_id=where,
                device_id_type=MESH,
            ).start()
            return carry

        lax.fori_loop(1, devices, start, 0, unroll=True)

        def finish():
            every = target.at[pl.ds(0, devices - 1)]
            pltpu.make_async_copy(every, every, send_sem.at[phase]).wait()
            pltpu.make_async_copy(every, every, recv_sem.at[phase]).wait()

        return finish

    loads[0].wait()
    index_row = jnp.concatenate(
        [index_ref[...], jnp.zeros((1, LANES - own_active), jnp.int32)], axis=1
    )
    index_all[me] = pltpu.roll(index_row, own_active * lax.rem(me, per_block), 1)
    pl.semaphore_wait(barrier, devices - 1)
    finish_index = exchange(0, lambda peer: index_all.at[me], index_all)

    for load in loads[1:]:
        load.wait()
    piece = 1024

    def prepare(which, carry):
        at = pl.ds(pl.multiple_of(which * piece, piece), piece)
        old_pos, old_vel, old_acc, old_jerk = (
            ref[:, at] for ref in (pos_ref, vel_ref, acc_ref, jerk_ref)
        )
        mass, elapsed = mass_ref[:, at], time_ref[:, at]
        pred_pos, pred_vel = predict(old_pos, old_vel, old_acc, old_jerk, elapsed)
        rows = padded([old_pos, old_vel, old_acc, old_jerk, elapsed], 16)
        packed[:, at] = padded(split3(rows), DEEP).astype(BF16)
        moments = padded([mass * pred_pos, mass * pred_vel, mass], 8)
        field[:, at] = padded(split3(moments), 32).astype(BF16)
        pos_parts, vel_parts = split3(pred_pos), split3(pred_vel)
        dot_parts = split3(jnp.sum(pred_pos * pred_vel, axis=0, keepdims=True))
        ones = jnp.ones((1, piece), F32)
        lhs = [pos_parts[right] for _, right in PARTS] + [vel_parts[right] for _, right in PARTS]
        lhs = padded(lhs + list(dot_parts) + [ones] * 3, 48)
        lhs = padded([lhs, pred_pos], DEEP)
        for part in range(piece // LANES):
            turned = jnp.transpose(lhs[:, part * LANES : (part + 1) * LANES])
            down = pl.ds(pl.multiple_of(which * piece + part * LANES, LANES), LANES)
            motion_lhs[down, :] = turned.astype(BF16)
            for axis in range(3):
                star_pos[axis, down, :] = jnp.broadcast_to(
                    turned[:, 48 + axis : 49 + axis], (LANES, LANES)
                )
        return carry

    lax.fori_loop(0, own_stars // piece, prepare, 0)

    finish_index()
    first = me * own_stars
    local = [
        jnp.sum(index_all[block * per_block : (block + 1) * per_block], axis=0) - first
        for block in range(lane_blocks)
    ]

    wide = 256
    tile = min(ROWS, active)
    across = tile // LANES
    down_16 = lax.broadcasted_iota(jnp.int32, (16, LANES), 0)
    picked[...] = jnp.zeros((DEEP, active), F32)

    for block in range(active // tile):
        columns = slice(block * tile, (block + 1) * tile)

        def pick(which, carry):
            base = which * wide
            at = pl.ds(pl.multiple_of(base, wide), wide)
            mine = [local[block * across + part] - base for part in range(across)]
            chosen = jnp.concatenate(
                [
                    jnp.concatenate(
                        [
                            jnp.where(down_16 == one - row, 1.0, 0.0).astype(BF16)
                            for row in range(0, wide, 16)
                        ],
                        axis=0,
                    )
                    for one in mine
                ],
                axis=1,
            )
            picked[:, columns] += jnp.dot(packed[:, at], chosen, preferred_element_type=F32)
            return carry

        lax.fori_loop(0, own_stars // wide, pick, 0)

    for block in range(lane_blocks):
        turned = picked[:, block * LANES : (block + 1) * LANES]
        rows = turned[0:16] + turned[16:32] + turned[32:48]
        for pair in range(per_block):
            send_state[block * per_block + pair] = rows[2 * pair : 2 * pair + 2]
    recv_state[me] = send_state[me]
    exchange(1, lambda peer: send_state.at[peer], recv_state)()
    state_all[me] = jnp.sum(recv_state[...], axis=0)
    exchange(2, lambda peer: state_all.at[me], state_all)()

    for block in range(lane_blocks):
        for pair in range(per_block):
            state[block, 2 * pair : 2 * pair + 2, :] = state_all[block * per_block + pair]
    for block in range(lane_blocks):
        rows = state[block]
        pred_pos, pred_vel = predict(rows[0:3], rows[3:6], rows[6:9], rows[9:12], rows[12:13])
        pos_parts, vel_parts = split3(-pred_pos), split3(-pred_vel)
        dot_parts = split3(jnp.sum(pred_pos * pred_vel, axis=0, keepdims=True))
        ones = jnp.ones((1, LANES), F32)
        lhs = [vel_parts[left] for left, _ in PARTS] + [pos_parts[left] for left, _ in PARTS]
        lhs = padded(lhs + [ones] * 3 + list(dot_parts), DEEP)
        rows_rhs[:, block * LANES : (block + 1) * LANES] = lhs.astype(BF16)
        rows_pos[:, block * LANES : (block + 1) * LANES] = padded([pred_pos], 8)

    chunks = own_stars // CHUNK

    def pair_weights(first_row, which, target):
        at = pl.multiple_of(which * CHUNK, CHUNK)
        mine = [
            [
                rows_pos[axis : axis + 1, first_row + lane : first_row + lane + LANES]
                for axis in range(3)
            ]
            for lane in range(0, tile, LANES)
        ]
        along = jnp.dot(
            motion_lhs[pl.ds(at, CHUNK), :],
            rows_rhs[:, first_row : first_row + tile],
            preferred_element_type=F32,
        )
        high = 16
        for row in range(0, CHUNK, high):
            stars = [star_pos[axis, pl.ds(at + row, high), :] for axis in range(3)]
            for lane in range(0, tile, LANES):
                squares = []
                for axis in range(3):
                    offset = stars[axis] - mine[lane // LANES][axis]
                    squares.append(offset * offset)
                inverse = lax.rsqrt(squares[0] + squares[1] + squares[2] + softening)
                inverse_sq = inverse * inverse
                cubed = inverse_sq * inverse
                slope = cubed * (inverse_sq * along[row : row + high, lane : lane + LANES])
                for number, value in enumerate((cubed, slope)):
                    near = value.astype(BF16)
                    far = (value - near.astype(F32)).astype(BF16)
                    start = 2 * number * CHUNK + row
                    target[start : start + high, lane : lane + LANES] = near
                    start += CHUNK
                    target[start : start + high, lane : lane + LANES] = far

    def add_up(first_row, which, source):
        at = pl.ds(pl.multiple_of(which * CHUNK, CHUNK), CHUNK)
        twice = jnp.concatenate([field[:, at]] * 2, axis=1)
        for number in range(2):
            sums[number, :, first_row : first_row + tile] += jnp.dot(
                twice,
                source[2 * number * CHUNK : 2 * (number + 1) * CHUNK, :],
                preferred_element_type=F32,
            )

    sums[...] = jnp.zeros((2, 32, active), F32)
    for block in range(active // tile):
        first_row = block * tile
        pair_weights(first_row, 0, weights_a)

        def advance(which, carry):
            pair_weights(first_row, 2 * which + 1, weights_b)
            add_up(first_row, 2 * which, weights_a)
            pair_weights(first_row, lax.rem(2 * which + 2, chunks), weights_a)
            add_up(first_row, 2 * which + 1, weights_b)
            return carry

        lax.fori_loop(0, chunks // 2, advance, 0)

    gravity = 1.0 / total_stars
    for block in range(lane_blocks):
        turned = sums[0, :, block * LANES : (block + 1) * LANES]
        plain = turned[0:8] + turned[8:16] + turned[16:24]
        turned = sums[1, :, block * LANES : (block + 1) * LANES]
        sloped = turned[0:8] + turned[8:16] + turned[16:24]
        rows = state[block]
        pred_pos, pred_vel = predict(rows[0:3], rows[3:6], rows[6:9], rows[9:12], rows[12:13])
        accel = plain[0:3] - pred_pos * plain[6:7]
        jerk = (plain[3:6] - pred_vel * plain[6:7]) - 3.0 * (
            sloped[0:3] - pred_pos * sloped[6:7]
        )
        send_force[block] = padded([accel, jerk], 8)
    mine = me // per_block
    recv_force[me] = send_force[mine]
    exchange(3, lambda peer: send_force.at[peer // per_block], recv_force)()
    forces = jnp.sum(recv_force[...], axis=0) * gravity
    rows = state[mine]
    shift = lax.rem(LANES - own_active * lax.rem(me, per_block), LANES)
    forces = pltpu.roll(forces, shift, 1)
    rows = pltpu.roll(rows, shift, 1)
    new_acc, new_jerk = forces[0:3], forces[3:6]
    old_pos, old_vel, old_acc, old_jerk = rows[0:3], rows[3:6], rows[6:9], rows[9:12]
    elapsed = rows[12:13]
    squared = elapsed * elapsed / 12.0
    new_vel = old_vel + 0.5 * elapsed * (old_acc + new_acc) + squared * (old_jerk - new_jerk)
    new_pos = old_pos + 0.5 * elapsed * (old_vel + new_vel) + squared * (old_acc - new_acc)
    for number, value in enumerate((new_pos, new_vel, new_acc, new_jerk)):
        result[number] = value[:, :own_active]


def hand_out(result, out_pos, out_vel, out_acc, out_jerk):
    for number, out in enumerate((out_pos, out_vel, out_acc, out_jerk)):
        out[...] = result[number]


def solution(mesh):
    blocks, groups = mesh.shape["blk"], mesh.shape["group"]
    devices = blocks * groups

    def on_device(positions, velocities, accelerations, jerk_rates, masses, elapsed_time, active_index):
        own_stars = positions.shape[1]
        own_active = active_index.shape[0]
        active = devices * own_active
        lane_blocks = active // LANES
        tile = min(ROWS, active)
        out = jax.ShapeDtypeStruct((3, own_active), F32)
        vmem = pl.BlockSpec(memory_space=pltpu.VMEM)
        result = pl.pallas_call(
            functools.partial(kernel, blocks, groups, own_stars * devices),
            out_shape=jax.ShapeDtypeStruct((4, 3, own_active), F32),
            in_specs=[pl.BlockSpec(memory_space=pltpu.HBM)] * 7,
            out_specs=vmem,
            scratch_shapes=[
                pltpu.VMEM((3, own_stars), F32),
                pltpu.VMEM((3, own_stars), F32),
                pltpu.VMEM((3, own_stars), F32),
                pltpu.VMEM((3, own_stars), F32),
                pltpu.VMEM((1, own_stars), F32),
                pltpu.VMEM((1, own_stars), F32),
                pltpu.VMEM((1, own_active), jnp.int32),
                pltpu.VMEM((devices, 1, LANES), jnp.int32),
                pltpu.VMEM((DEEP, own_stars), BF16),
                pltpu.VMEM((32, own_stars), BF16),
                pltpu.VMEM((own_stars, DEEP), BF16),
                pltpu.VMEM((3, own_stars, LANES), F32),
                pltpu.VMEM((DEEP, active), F32),
                pltpu.VMEM((devices, 2, LANES), F32),
                pltpu.VMEM((devices, 2, LANES), F32),
                pltpu.VMEM((devices, 2, LANES), F32),
                pltpu.VMEM((lane_blocks, 16, LANES), F32),
                pltpu.VMEM((DEEP, active), BF16),
                pltpu.VMEM((8, active), F32),
                pltpu.VMEM((4 * CHUNK, tile), BF16),
                pltpu.VMEM((4 * CHUNK, tile), BF16),
                pltpu.VMEM((2, 32, active), F32),
                pltpu.VMEM((lane_blocks, 8, LANES), F32),
                pltpu.VMEM((devices, 8, LANES), F32),
                pltpu.SemaphoreType.DMA((4,)),
                pltpu.SemaphoreType.DMA((4,)),
                pltpu.SemaphoreType.DMA((7,)),
            ],
            compiler_params=pltpu.CompilerParams(
                collective_id=0, has_side_effects=True, vmem_limit_bytes=56 * 1024 * 1024
            ),
            cost_estimate=pl.CostEstimate(
                flops=40 * active * own_stars, bytes_accessed=4 * 14 * own_stars,
                transcendentals=active * own_stars,
            ),
        )(
            positions, velocities, accelerations, jerk_rates,
            masses.reshape(1, own_stars), elapsed_time.reshape(1, own_stars),
            active_index.reshape(1, own_active),
        )
        return pl.pallas_call(
            hand_out, out_shape=(out,) * 4, in_specs=[vmem], out_specs=(vmem,) * 4
        )(result)

    wide = P(None, ("blk", "group"))
    flat = P(("blk", "group"))
    return jax.shard_map(
        on_device,
        mesh=mesh,
        in_specs=(wide, wide, wide, wide, flat, flat, flat),
        out_specs=(wide,) * 4,
        check_vma=False,
    )
```
